32 devices in a mesh: basin: 2 (over y), tm: 16 (over z, x, core).
Axes of the slice: x: 2, y: 2, z: 4, core: 2. Of those that a mesh axis runs over, the one named last changes fastest.
Arguments:
- perturbation: bfloat16 [64, 512, 512], P(('basin', 'tm')), parts along dimension 0, may hold values from -0.02734375 to 0.02734375
- hours_live: int32 [32], P(('basin', 'tm')), parts along dimension 0, may hold values from 1 to 2, as said below
- start_hour: int32 [1], replicated, may hold values from 0 to 15
- release_coeffs: bfloat16 [1024, 2048], P('basin'), parts along dimension 0, may hold values from -6 to 6
- batch_of_column: int32 [4096], P('basin'), parts along dimension 0, may hold values from 0 to 63
- batch_amplitude: float32 [128], P('basin'), parts along dimension 0, may hold values from 0.1 to 3
Outputs:
- panels: bfloat16 [32, 512, 2048], P(('basin', 'tm')), parts along dimension 0
The draws below stay inside these ranges and needn't reach their ends.
There are 2 independent parts, one for each index of `basin`. The reference program is written for one: setup_inputs(seed, part) draws one part's arguments, and reference() takes and returns one part's arrays. A program takes and returns all parts, laid end to end along the dimension named above; an argument that names none is the same for every part. Nothing has to cross between parts.
Inputs may be any that keep to these rules, and one draw needn't show every extreme that they name: `hours_live`: some owner has all 2 hours live.
All inputs are finite; a program needn't handle non-finite values.
Results may differ from the reference program's by a relative error of at most 0.0057.
Values sent between devices are 32-bit elements; how exact they have to be, the bound alone decides.
A program may use at most 64 MiB of HBM per device.

```python
import math
import jax
import jax.numpy as jnp
from jax import lax

R = 512
C = 2048
NB = 64
HOURS_DEV = 2
OWNERS = 16
HOURS = 32


def draw_hours_live(key, part):
    key = jax.random.fold_in(key, 5)
    first_key, second_key = jax.random.split(key)
    counts = jax.random.randint(first_key, (OWNERS,), 1, HOURS_DEV + 1)
    where = jax.random.randint(second_key, (), 0, OWNERS)
    return jnp.where(jnp.arange(OWNERS) == where, HOURS_DEV, counts).astype(jnp.int32)


def plant(array, key, low, high):
    shape = array.shape
    place = [jax.random.randint(jax.random.fold_in(key, axis), (), 0, shape[axis]) for axis in range(len(shape))]
    array = array.at[tuple(place)].set(low)
    longest = shape.index(max(shape))
    place[longest] = (place[longest] + 1) % shape[longest]
    return array.at[tuple(place)].set(high)


def steps_of(stream_key, extent, cuts, smallest, top_value):
    def one(axis_at, blocks):
        draws = jax.random.uniform(jax.random.fold_in(jax.random.fold_in(stream_key, 6), axis_at), (blocks,), jnp.float32, smallest / len(cuts), top_value / len(cuts))
        return jnp.repeat(jnp.exp(draws), extent[axis_at] // blocks).reshape((-1,) + (1,) * (len(extent) - axis_at - 1))

    level = one(*cuts[0])
    for cut in cuts[1:]:
        level = level * one(*cut)
    return level


def normal_values(stream_key, shape, width, bound, cuts=(), held_as=jnp.bfloat16):
    values = width * jax.random.normal(stream_key, shape, jnp.float32)
    if cuts:
        values = values * steps_of(stream_key, shape, cuts, -0.22, 0.18)
    return jnp.clip(values, -bound, bound).astype(held_as)


def setup_inputs(seed: int = 0, part: int = 0) -> dict:
    splits = jax.random.split(jax.random.key(seed), 7)
    part_splits = jax.random.split(jax.random.fold_in(splits[6], part), 7)
    perturbation = normal_values(part_splits[0], (HOURS, R, R), (100 * R) ** -0.5, 0.02734375, ((0, 16),))
    hours_live = draw_hours_live(jax.random.fold_in(jax.random.fold_in(splits[6], part), 71), part)
    start_hour = jax.random.randint(splits[2], (1,), 0, HOURS // 2).astype(jnp.int32)
    release_coeffs = normal_values(part_splits[3], (R, C), 1.0, 6.0)
    batch_of_column = plant(jax.random.randint(part_splits[4], (C,), 0, NB), jax.random.fold_in(part_splits[4], 1), 0, NB - 1).astype(jnp.int32)
    batch_amplitude = jnp.clip(jnp.exp(jax.random.uniform(part_splits[5], (NB,), jnp.float32, math.log(0.1), math.log(3.0))), 0.1, 3.0)
    return {"perturbation": perturbation, "hours_live": hours_live, "start_hour": start_hour, "release_coeffs": release_coeffs, "batch_of_column": batch_of_column, "batch_amplitude": batch_amplitude}


def own_product(pieces, live_count, owner, start, hours_dev):
    order = pieces.shape[1]
    eye = jnp.eye(order, dtype=jnp.float32)
    total = eye
    for j in range(hours_dev):
        hour = owner * hours_dev + j
        alive = jnp.logical_and(j < live_count, hour >= start)
        operator = eye + jnp.where(alive, pieces[j].astype(jnp.float32), jnp.float32(0.0))
        total = jnp.dot(operator, total, precision=lax.Precision.HIGHEST, preferred_element_type=jnp.float32)
    return total


def make_release(release_coeffs, batch_of_column, batch_amplitude):
    match = batch_of_column[:, None] == jnp.arange(batch_amplitude.shape[0], dtype=jnp.int32)[None, :]
    column_scale = jnp.sum(jnp.where(match, batch_amplitude[None, :], jnp.float32(0.0)), axis=1)
    return (release_coeffs.astype(jnp.float32) * column_scale[None, :]).astype(jnp.bfloat16)


def reference(perturbation, hours_live, start_hour, release_coeffs, batch_of_column, batch_amplitude):
    release = make_release(release_coeffs, batch_of_column, batch_amplitude)
    stacked = perturbation.reshape(OWNERS, HOURS_DEV, R, R)
    start = start_hour[0]

    def step(carry, inputs):
        pieces, live_count, owner = inputs
        local = own_product(pieces, live_count, owner, start, HOURS_DEV)
        reach = jnp.dot(local, carry, precision=lax.Precision.HIGHEST, preferred_element_type=jnp.float32)
        panel = jnp.dot(reach.astype(jnp.bfloat16), release, preferred_element_type=jnp.float32).astype(jnp.bfloat16)
        return reach, panel

    owners = jnp.arange(OWNERS, dtype=jnp.int32)
    first = jnp.eye(R, dtype=jnp.float32)
    last, panels = lax.scan(step, first, (stacked, hours_live, owners))
    return panels
```

```python
import functools
import jax
import jax.numpy as jnp
from jax import lax
from jax.experimental import pallas as pl
from jax.experimental.pallas import tpu as pltpu
from jax.sharding import PartitionSpec as P

MESH = pl.DeviceIdType.MESH
QUAD = 4
X_CHUNKS = 4
CHAIN_CHUNKS = 4


def halves(value):
    high = value.astype(jnp.bfloat16)
    return high, (value - high.astype(jnp.float32)).astype(jnp.bfloat16)


def mul(a, b):
    return jnp.dot(a, b, preferred_element_type=jnp.float32)


def times(left, right, right_high, right_low):
    high, low = halves(left)
    return left + right + (mul(high, right_high) + (mul(high, right_low) + mul(low, right_high)))


def kernel(
    count,
    hours_live,
    start_hour,
    pert,
    coeffs,
    batch,
    amplitude,
    panel,
    local2,
    chip2,
    quad,
    reach_in,
    within,
    sent,
    right_high,
    right_low,
    quad_high,
    quad_low,
    release,
    reach_out,
    core_sem,
    x_sem,
    xf_sem,
    z_sem,
    ef_sem,
    ex_sem,
    exf_sem,
):
    order = pert.shape[1]
    me = lax.axis_index("tm")
    core = me % 2
    x = (me // 2) % 2
    lane = me % QUAD
    q = me // QUAD
    quads = count // QUAD
    core_mate = me + 1 - 2 * core
    x_mate = me + 2 - 4 * x
    has_next = q < quads - 1
    has_prev = q > 0

    barrier = pltpu.get_barrier_semaphore()
    for mate in (core_mate, x_mate):
        pl.semaphore_signal(barrier, inc=1, device_id={"tm": mate}, device_id_type=MESH)

    @pl.when(has_next)
    def _():
        pl.semaphore_signal(barrier, inc=1, device_id={"tm": me + QUAD}, device_id_type=MESH)

    @pl.when(has_prev)
    def _():
        pl.semaphore_signal(barrier, inc=1, device_id={"tm": me - QUAD}, device_id_type=MESH)

    scales = []
    for j in range(pert.shape[0]):
        alive = jnp.logical_and(j < hours_live[0], me * pert.shape[0] + j >= start_hour[0])
        scales.append(jnp.where(alive, jnp.float32(1.0), jnp.float32(0.0)))
    total = pert[0].astype(jnp.float32) * scales[0]
    for j in range(1, pert.shape[0]):
        left = pert[j].astype(jnp.float32) * scales[j]
        high, low = halves(total)
        factor = left.astype(jnp.bfloat16)
        product = mul(factor, high)
        if j > 1:
            product = product + mul(factor, low)
        total = total + left + product
    local2[core] = total.T

    pl.semaphore_wait(barrier, 2 + has_next.astype(jnp.int32) + has_prev.astype(jnp.int32))

    def remote(src, dst, send, recv, device):
        return pltpu.make_async_remote_copy(
            src_ref=src,
            dst_ref=dst,
            send_sem=send,
            recv_sem=recv,
            device_id={"tm": device},
            device_id_type=MESH,
        )

    to_core = remote(
        local2.at[core], local2.at[core], core_sem.at[0], core_sem.at[1], core_mate
    )
    to_core.start()
    to_core.wait()

    high, low = halves(local2[1])
    right_high[...] = high
    right_low[...] = low
    half = order // 2
    step = half // X_CHUNKS

    def x_rows(c, s):
        return pl.ds(pl.multiple_of(c * half + s * step, step), step)

    def chip_rows(rows):
        chip2[x, rows] = times(local2[0, rows], local2[1, rows], right_high[...], right_low[...])

    def x_copy(s):
        rows = x_rows(core, s)
        return remote(
            chip2.at[x, rows], chip2.at[x, rows], x_sem.at[0, s], x_sem.at[1, s], x_mate
        )

    def x_forward(s):
        rows = x_rows(core, s)
        return remote(
            chip2.at[1 - x, rows],
            chip2.at[1 - x, rows],
            xf_sem.at[0, s],
            xf_sem.at[1, s],
            core_mate,
        )

    for s in range(X_CHUNKS):
        chip_rows(x_rows(core, s))
        x_copy(s).start()
    chip_rows(pl.ds(pl.multiple_of((1 - core) * half, half), half))

    ids = lax.broadcasted_iota(jnp.int32, (amplitude.shape[0], batch.shape[1]), 0)
    column_scale = jnp.sum(
        jnp.where(ids == batch[...], amplitude[...], jnp.float32(0.0)), axis=0, keepdims=True
    )
    release[...] = (coeffs[...].astype(jnp.float32) * column_scale).astype(jnp.bfloat16)

    for s in range(X_CHUNKS):
        x_copy(s).wait_recv()
        x_forward(s).start()
    for s in range(X_CHUNKS):
        x_forward(s).wait_recv()

    high, low = halves(chip2[1])
    right_high[...] = high
    right_low[...] = low
    quad[...] = times(chip2[0], chip2[1], right_high[...], right_low[...])
    high, low = halves(quad[...])
    quad_high[...] = high
    quad_low[...] = low

    share = order // QUAD
    part = share // CHAIN_CHUNKS

    def lane_rows(which, s):
        return pl.ds(pl.multiple_of(which * share + s * part, part), part)

    def chain(s):
        return remote(
            sent.at[pl.ds(s * part, part)],
            reach_in.at[lane_rows(lane, s)],
            z_sem.at[0, s],
            z_sem.at[1, s],
            me + QUAD,
        )

    def to_mate(sem, which, device, s):
        rows = lane_rows(which, s)
        return remote(reach_in.at[rows], reach_in.at[rows], sem.at[0, s], sem.at[1, s], device)

    own_core = functools.partial(to_mate, ef_sem, lane, core_mate)
    own_x = functools.partial(to_mate, ex_sem, lane, x_mate)
    x_lane = lane + 2 - 4 * x
    other_core = functools.partial(to_mate, exf_sem, x_lane, core_mate)

    @pl.when(q == 0)
    def _():
        reach_in[...] = jnp.zeros_like(reach_in)

    def chain_step(s):
        rows = lane_rows(lane, s)

        @pl.when(has_prev)
        def _():
            chain(s).wait_recv()
            own_x(s).start()
            own_core(s).start()

        @pl.when(has_next)
        def _():
            sent[s * part : (s + 1) * part] = times(
                reach_in[rows], quad[rows], quad_high[...], quad_low[...]
            )
            chain(s).start()

    def share_step(s):
        @pl.when(has_prev)
        def _():
            to_mate(ex_sem, x_lane, x_mate, s).wait_recv()
            other_core(s).start()

    for s in range(CHAIN_CHUNKS):
        chain_step(s)
        if s:
            share_step(s - 1)

    @pl.when(lane == 0)
    def _():
        within[...] = local2[0]

    @pl.when(lane == 1)
    def _():
        within[...] = chip2[0]

    @pl.when(lane == 2)
    def _():
        high, low = halves(local2[0])
        within[...] = times(chip2[0], local2[0], high, low)

    @pl.when(lane == 3)
    def _():
        within[...] = quad[...]

    high, low = halves(within[...])
    right_high[...] = high
    right_low[...] = low
    share_step(CHAIN_CHUNKS - 1)

    @pl.when(has_prev)
    def _():
        for s in range(CHAIN_CHUNKS):
            to_mate(ef_sem, lane + 1 - 2 * core, core_mate, s).wait_recv()
            to_mate(exf_sem, x_lane + 1 - 2 * core, core_mate, s).wait_recv()

    diagonal = lax.broadcasted_iota(jnp.int32, (order, order), 0) == lax.broadcasted_iota(
        jnp.int32, (order, order), 1
    )
    reach = times(reach_in[...], within[...], right_high[...], right_low[...])
    reach = reach + jnp.where(diagonal, jnp.float32(1.0), jnp.float32(0.0))
    reach_out[...] = reach.T.astype(jnp.bfloat16)
    width = panel.shape[2] // 4
    for s in range(4):
        columns = slice(s * width, (s + 1) * width)
        panel[0, :, columns] = mul(reach_out[...], release[:, columns]).astype(jnp.bfloat16)

    for s in range(X_CHUNKS):
        x_copy(s).wait_send()
        x_forward(s).wait_send()
    for s in range(CHAIN_CHUNKS):

        @pl.when(has_next)
        def _():
            chain(s).wait_send()

        @pl.when(has_prev)
        def _():
            own_x(s).wait_send()
            own_core(s).wait_send()
            other_core(s).wait_send()


def on_device(
    count, perturbation, hours_live, start_hour, release_coeffs, batch_of_column, batch_amplitude
):
    order = perturbation.shape[1]
    columns = release_coeffs.shape[1]
    vmem = pl.BlockSpec(memory_space=pltpu.VMEM)
    smem = pl.BlockSpec(memory_space=pltpu.SMEM)
    f32, bf16 = jnp.float32, jnp.bfloat16
    square = (order, order)
    return pl.pallas_call(
        functools.partial(kernel, count),
        out_shape=jax.ShapeDtypeStruct((1, order, columns), bf16),
        in_specs=[smem, smem, vmem, vmem, vmem, vmem],
        out_specs=vmem,
        scratch_shapes=[
            pltpu.VMEM((2,) + square, f32),
            pltpu.VMEM((2,) + square, f32),
            pltpu.VMEM(square, f32),
            pltpu.VMEM(square, f32),
            pltpu.VMEM(square, f32),
            pltpu.VMEM((order // QUAD, order), f32),
            pltpu.VMEM(square, bf16),
            pltpu.VMEM(square, bf16),
            pltpu.VMEM(square, bf16),
            pltpu.VMEM(square, bf16),
            pltpu.VMEM((order, columns), bf16),
            pltpu.VMEM(square, bf16),
            pltpu.SemaphoreType.DMA((2,)),
            pltpu.SemaphoreType.DMA((2, X_CHUNKS)),
            pltpu.SemaphoreType.DMA((2, X_CHUNKS)),
            pltpu.SemaphoreType.DMA((2, CHAIN_CHUNKS)),
            pltpu.SemaphoreType.DMA((2, CHAIN_CHUNKS)),
            pltpu.SemaphoreType.DMA((2, CHAIN_CHUNKS)),
            pltpu.SemaphoreType.DMA((2, CHAIN_CHUNKS)),
        ],
        compiler_params=pltpu.CompilerParams(
            collective_id=0, has_side_effects=True, vmem_limit_bytes=48 * 1024 * 1024
        ),
    )(
        hours_live,
        start_hour,
        perturbation,
        release_coeffs,
        batch_of_column[None, :],
        batch_amplitude[:, None],
    )


def solution(mesh):
    in_specs = (
        P(("basin", "tm"), None, None),
        P(("basin", "tm")),
        P(),
        P("basin", None),
        P("basin"),
        P("basin"),
    )
    out_specs = P(("basin", "tm"), None, None)
    return jax.shard_map(
        functools.partial(on_device, mesh.shape["tm"]),
        mesh=mesh,
        in_specs=in_specs,
        out_specs=out_specs,
        check_vma=False,
    )
```

```python
import functools
import jax
import jax.numpy as jnp
from jax import lax
from jax.experimental import pallas as pl
from jax.experimental.pallas import tpu as pltpu
from jax.sharding import PartitionSpec as P

MESH = pl.DeviceIdType.MESH
QUAD = 4
UNITS = 32


def halves(value):
    high = value.astype(jnp.bfloat16)
    return high, (value - high.astype(jnp.float32)).astype(jnp.bfloat16)


def mul(a, b):
    return jnp.dot(a, b, preferred_element_type=jnp.float32)


def times(left, right, right_high, right_low):
    high, low = halves(left)
    return left + right + (mul(high, right_high) + (mul(high, right_low) + mul(low, right_high)))


def kernel(
    count,
    hours_live,
    start_hour,
    amplitude,
    pert_in,
    coeffs_in,
    batch_in,
    reach_out,
    release,
    pert,
    coeffs,
    batch,
    local2,
    chip2,
    quad,
    reach_in,
    within,
    sent,
    back,
    right_high,
    right_low,
    quad_high,
    quad_low,
    in_sem,
    core_sem,
    x_sem,
    xf_sem,
    back_sem,
    z_sem,
    ef_sem,
    ex_sem,
    exf_sem,
):
    order = pert.shape[1]
    unit = order // UNITS
    per_core = UNITS // 2
    per_lane = UNITS // QUAD
    me = lax.axis_index("tm")
    core = me % 2
    x = (me // 2) % 2
    lane = me % QUAD
    q = me // QUAD
    core_mate = me + 1 - 2 * core
    x_mate = me + 2 - 4 * x
    has_next = q < count // QUAD - 1
    has_prev = q > 0
    first = q == 0
    gets_x = jnp.logical_or(has_prev, x == 1)
    sends_x = jnp.logical_or(has_prev, x == 0)

    fetches = [
        pltpu.make_async_copy(src, dst, in_sem.at[i])
        for i, (src, dst) in enumerate(((pert_in, pert), (coeffs_in, coeffs), (batch_in, batch)))
    ]
    for fetch in fetches:
        fetch.start()
    barrier = pltpu.get_barrier_semaphore()
    for mate in (core_mate, x_mate):
        pl.semaphore_signal(barrier, inc=1, device_id={"tm": mate}, device_id_type=MESH)

    @pl.when(has_next)
    def _():
        pl.semaphore_signal(barrier, inc=1, device_id={"tm": me + QUAD}, device_id_type=MESH)

    @pl.when(has_prev)
    def _():
        pl.semaphore_signal(barrier, inc=1, device_id={"tm": me - QUAD}, device_id_type=MESH)

    scales = []
    for j in range(pert.shape[0]):
        alive = jnp.logical_and(j < hours_live[0], me * pert.shape[0] + j >= start_hour[0])
        scales.append(jnp.where(alive, jnp.float32(1.0), jnp.float32(0.0)))
    fetches[0].wait()
    total = pert[0].astype(jnp.float32) * scales[0]
    for j in range(1, pert.shape[0]):
        left = pert[j].astype(jnp.float32) * scales[j]
        high, low = halves(total)
        factor = left.astype(jnp.bfloat16)
        product = mul(factor, high)
        if j > 1:
            product = product + mul(factor, low)
        total = total + left + product
    local2[core] = total.T

    pl.semaphore_wait(barrier, 2 + has_next.astype(jnp.int32) + has_prev.astype(jnp.int32))

    def remote(src, dst, sems, i, device):
        return pltpu.make_async_remote_copy(
            src_ref=src,
            dst_ref=dst,
            send_sem=sems.at[0, i],
            recv_sem=sems.at[1, i],
            device_id={"tm": device},
            device_id_type=MESH,
        )

    def same(ref, sems, i, device):
        return remote(ref, ref, sems, i, device)

    def rows_at(chunk):
        return pl.ds(pl.multiple_of(chunk * unit, unit), unit)

    group = order // QUAD

    def to_core(owner, g):
        return same(local2.at[owner, pl.ds(g * group, group)], core_sem, g, core_mate)

    for g in range(QUAD):
        to_core(core, g).start()

    @pl.when(core == 0)
    def _():
        for g in range(QUAD):
            to_core(1 - core, g).wait_recv()

    high, low = halves(local2[1])
    right_high[...] = high
    right_low[...] = low

    def x_copy(side, c, j):
        return same(chip2.at[side, rows_at(2 * j + c)], x_sem, j, x_mate)

    def x_forward(c, j):
        return same(chip2.at[1 - x, rows_at(2 * j + c)], xf_sem, j, core_mate)

    for g in range(QUAD):

        @pl.when(core == 1)
        def _():
            to_core(1 - core, g).wait_recv()

        rows = slice(g * group, (g + 1) * group)
        chip2[x, rows] = times(local2[0, rows], local2[1, rows], right_high[...], right_low[...])

        @pl.when(sends_x)
        def _():
            for j in range(g * per_core // QUAD, (g + 1) * per_core // QUAD):
                x_copy(x, core, j).start()

    def make_release():
        fetches[1].wait()
        fetches[2].wait()
        ids = batch[...]
        column_scale = jnp.zeros(ids.shape, jnp.float32)
        for b in range(amplitude.shape[0]):
            column_scale = jnp.where(ids == b, amplitude[b], column_scale)
        release[...] = (coeffs[...].astype(jnp.float32) * column_scale).astype(jnp.bfloat16)

    pl.when(has_prev)(make_release)

    def send_back(s):
        here = pl.ds(pl.multiple_of(s * unit, unit), unit)
        return remote(back.at[here], sent.at[here], back_sem, s, x_mate)

    def chain(c_lane, s):
        here = pl.ds(pl.multiple_of(s * unit, unit), unit)
        chunk = (c_lane // 2) * per_core + 2 * s + c_lane % 2
        return remote(sent.at[here], reach_in.at[rows_at(chunk)], z_sem, s, me + QUAD)

    @pl.when(jnp.logical_and(first, x == 1))
    def _():
        high, low = halves(chip2[1])
        right_high[...] = high
        right_low[...] = low

        def step(j):
            x_copy(1 - x, core, j).wait_recv()
            x_forward(core, j).start()
            rows = rows_at(2 * j + core)
            return times(chip2[0, rows], chip2[1, rows], right_high[...], right_low[...])

        @pl.loop(0, per_lane)
        def _(j):
            back[pl.ds(pl.multiple_of(j * unit, unit), unit)] = step(j)
            send_back(j).start()

        @pl.loop(0, per_lane)
        def _(s):
            sent[pl.ds(pl.multiple_of(s * unit, unit), unit)] = step(s + per_lane)

            @pl.when(has_next)
            def _():
                chain(lane, s).start()

    @pl.when(jnp.logical_and(first, x == 0))
    def _():
        @pl.loop(0, per_lane)
        def _(s):
            send_back(s).wait_recv()

            @pl.when(has_next)
            def _():
                chain(lane, s).start()

    @pl.when(has_prev)
    def _():
        @pl.loop(0, per_core)
        def _(j):
            x_copy(1 - x, core, j).wait_recv()
            x_forward(core, j).start()

    pl.when(first)(make_release)

    @pl.when(gets_x)
    def _():
        @pl.loop(0, per_core)
        def _(j):
            x_forward(1 - core, j).wait_recv()

        high, low = halves(chip2[1])
        right_high[...] = high
        right_low[...] = low
        quad[...] = times(chip2[0], chip2[1], right_high[...], right_low[...])
        high, low = halves(quad[...])
        quad_high[...] = high
        quad_low[...] = low

    def make_within():
        @pl.when(lane == 0)
        def _():
            within[...] = local2[0]

        @pl.when(lane == 1)
        def _():
            within[...] = chip2[0]

        @pl.when(lane == 2)
        def _():
            high, low = halves(local2[0])
            within[...] = times(chip2[0], local2[0], high, low)

        @pl.when(lane == 3)
        def _():
            within[...] = quad[...]

        high, low = halves(within[...])
        right_high[...] = high
        right_low[...] = low

    pl.when(jnp.logical_not(has_next))(make_within)

    def lane_rows(c_lane, s):
        return rows_at((c_lane // 2) * per_core + 2 * s + c_lane % 2)

    def shared(sems, c_lane, device, s):
        return same(reach_in.at[lane_rows(c_lane, s)], sems, s, device)

    x_lane = lane + 2 - 4 * x
    core_lane = lane + 1 - 2 * core
    xc_lane = x_lane + 1 - 2 * core

    def share_x(s):
        shared(ex_sem, x_lane, x_mate, s).wait_recv()
        shared(exf_sem, x_lane, core_mate, s).start()

    @pl.when(has_prev)
    def _():
        @pl.loop(0, per_lane)
        def _(s):
            chain(lane, s).wait_recv()
            shared(ex_sem, lane, x_mate, s).start()
            shared(ef_sem, lane, core_mate, s).start()

            @pl.when(has_next)
            def _():
                rows = lane_rows(lane, s)
                sent[pl.ds(pl.multiple_of(s * unit, unit), unit)] = times(
                    reach_in[rows], quad[rows], quad_high[...], quad_low[...]
                )
                chain(lane, s).start()

            @pl.when(s > 1)
            def _():
                share_x(s - 2)

    pl.when(has_next)(make_within)

    def finish(value, start, size):
        shape = (size, order)
        diagonal = start + lax.broadcasted_iota(
            jnp.int32, shape, 0
        ) == lax.broadcasted_iota(jnp.int32, shape, 1)
        value = value + jnp.where(diagonal, jnp.float32(1.0), jnp.float32(0.0))
        reach_out[:, pl.ds(start, size)] = value.T.astype(jnp.bfloat16)

    @pl.when(first)
    def _():
        finish(within[...], 0, order)

    half = order // 2

    def finish_half(side):
        start = pl.multiple_of(side * half, half)
        rows = pl.ds(start, half)
        finish(
            times(reach_in[rows], within[rows], right_high[...], right_low[...]), start, half
        )

    @pl.when(has_prev)
    def _():
        share_x(per_lane - 2)
        share_x(per_lane - 1)

        @pl.loop(0, per_lane)
        def _(s):
            shared(ef_sem, core_lane, core_mate, s).wait_recv()

        finish_half(x)

        @pl.loop(0, per_lane)
        def _(s):
            shared(exf_sem, xc_lane, core_mate, s).wait_recv()

        finish_half(1 - x)

    for g in range(QUAD):
        to_core(core, g).wait_send()

    @pl.when(sends_x)
    def _():
        @pl.loop(0, per_core)
        def _(j):
            x_copy(x, core, j).wait_send()

    @pl.when(gets_x)
    def _():
        @pl.loop(0, per_core)
        def _(j):
            x_forward(core, j).wait_send()

    @pl.when(jnp.logical_and(first, x == 1))
    def _():
        @pl.loop(0, per_lane)
        def _(s):
            send_back(s).wait_send()

    @pl.when(has_next)
    def _():
        @pl.loop(0, per_lane)
        def _(s):
            chain(lane, s).wait_send()

    @pl.when(has_prev)
    def _():
        @pl.loop(0, per_lane)
        def _(s):
            shared(ex_sem, lane, x_mate, s).wait_send()
            shared(ef_sem, lane, core_mate, s).wait_send()
            shared(exf_sem, x_lane, core_mate, s).wait_send()


def on_device(
    count, perturbation, hours_live, start_hour, release_coeffs, batch_of_column, batch_amplitude
):
    order = perturbation.shape[1]
    columns = release_coeffs.shape[1]
    vmem = pl.BlockSpec(memory_space=pltpu.VMEM)
    smem = pl.BlockSpec(memory_space=pltpu.SMEM)
    anywhere = pl.BlockSpec(memory_space=pl.ANY)
    f32, bf16 = jnp.float32, jnp.bfloat16
    square = (order, order)
    sems = lambda n: pltpu.SemaphoreType.DMA((2, n))
    reach, release = pl.pallas_call(
        functools.partial(kernel, count),
        out_shape=(
            jax.ShapeDtypeStruct(square, bf16),
            jax.ShapeDtypeStruct((order, columns), bf16),
        ),
        in_specs=[smem, smem, smem, anywhere, anywhere, anywhere],
        out_specs=(vmem, vmem),
        scratch_shapes=[
            pltpu.VMEM(perturbation.shape, bf16),
            pltpu.VMEM((order, columns), bf16),
            pltpu.VMEM((1, columns), jnp.int32),
            pltpu.VMEM((2,) + square, f32),
            pltpu.VMEM((2,) + square, f32),
            pltpu.VMEM(square, f32),
            pltpu.VMEM(square, f32),
            pltpu.VMEM(square, f32),
            pltpu.VMEM((order // QUAD, order), f32),
            pltpu.VMEM((order // QUAD, order), f32),
            pltpu.VMEM(square, bf16),
            pltpu.VMEM(square, bf16),
            pltpu.VMEM(square, bf16),
            pltpu.VMEM(square, bf16),
            pltpu.SemaphoreType.DMA((3,)),
            sems(QUAD),
            sems(UNITS // 2),
            sems(UNITS // 2),
            sems(UNITS // QUAD),
            sems(UNITS // QUAD),
            sems(UNITS // QUAD),
            sems(UNITS // QUAD),
            sems(UNITS // QUAD),
        ],
        compiler_params=pltpu.CompilerParams(
            collective_id=0, has_side_effects=True, vmem_limit_bytes=48 * 1024 * 1024
        ),
    )(
        hours_live,
        start_hour,
        batch_amplitude,
        perturbation,
        release_coeffs,
        batch_of_column[None, :],
    )
    panel = jnp.dot(reach, release, preferred_element_type=jnp.float32)
    return panel.astype(bf16)[None, :, :]


def solution(mesh):
    in_specs = (
        P(("basin", "tm"), None, None),
        P(("basin", "tm")),
        P(),
        P("basin", None),
        P("basin"),
        P("basin"),
    )
    out_specs = P(("basin", "tm"), None, None)
    return jax.shard_map(
        functools.partial(on_device, mesh.shape["tm"]),
        mesh=mesh,
        in_specs=in_specs,
        out_specs=out_specs,
        check_vma=False,
    )
```

```python
import functools
import jax
import jax.numpy as jnp
from jax import lax
from jax.experimental import pallas as pl
from jax.experimental.pallas import tpu as pltpu
from jax.sharding import PartitionSpec as P

MESH = pl.DeviceIdType.MESH
QUAD = 4
UNITS = 32


def halves(value):
    high = value.astype(jnp.bfloat16)
    return high, (value - high.astype(jnp.float32)).astype(jnp.bfloat16)


def mul(a, b):
    return jnp.dot(a, b, preferred_element_type=jnp.float32)


def times(left, right, right_high, right_low):
    high, low = halves(left)
    return left + right + (mul(high, right_high) + (mul(high, right_low) + mul(low, right_high)))


def kernel(
    count,
    hours_live,
    start_hour,
    amplitude,
    pert_in,
    coeffs_in,
    batch_in,
    reach_out,
    release_out,
    release,
    pert,
    coeffs,
    batch,
    local2,
    chip2,
    quad,
    reach_in,
    within,
    sent,
    back,
    right_high,
    right_low,
    quad_high,
    quad_low,
    in_sem,
    core_sem,
    x_sem,
    xf_sem,
    back_sem,
    z_sem,
    ef_sem,
    ex_sem,
    exf_sem,
):
    order = pert.shape[1]
    unit = order // UNITS
    per_core = UNITS // 2
    per_lane = UNITS // QUAD
    me = lax.axis_index("tm")
    core = me % 2
    x = (me // 2) % 2
    lane = me % QUAD
    q = me // QUAD
    core_mate = me + 1 - 2 * core
    x_mate = me + 2 - 4 * x
    has_next = q < count // QUAD - 1
    has_prev = q > 0
    first = q == 0
    gets_x = jnp.logical_or(has_prev, x == 1)
    sends_x = jnp.logical_or(has_prev, x == 0)

    fetches = [
        pltpu.make_async_copy(src, dst, in_sem.at[i])
        for i, (src, dst) in enumerate(((pert_in, pert), (coeffs_in, coeffs), (batch_in, batch)))
    ]
    for fetch in fetches:
        fetch.start()
    store = pltpu.make_async_copy(release, release_out, in_sem.at[3])
    barrier = pltpu.get_barrier_semaphore()
    for mate in (core_mate, x_mate):
        pl.semaphore_signal(barrier, inc=1, device_id={"tm": mate}, device_id_type=MESH)

    @pl.when(has_next)
    def _():
        pl.semaphore_signal(barrier, inc=1, device_id={"tm": me + QUAD}, device_id_type=MESH)

    @pl.when(has_prev)
    def _():
        pl.semaphore_signal(barrier, inc=1, device_id={"tm": me - QUAD}, device_id_type=MESH)

    scales = []
    for j in range(pert.shape[0]):
        alive = jnp.logical_and(j < hours_live[0], me * pert.shape[0] + j >= start_hour[0])
        scales.append(jnp.where(alive, jnp.float32(1.0), jnp.float32(0.0)))
    fetches[0].wait()
    total = pert[0].astype(jnp.float32) * scales[0]
    for j in range(1, pert.shape[0]):
        left = pert[j].astype(jnp.float32) * scales[j]
        high, low = halves(total)
        factor = left.astype(jnp.bfloat16)
        product = mul(factor, high)
        if j > 1:
            product = product + mul(factor, low)
        total = total + left + product
    local2[core] = total.T

    pl.semaphore_wait(barrier, 2 + has_next.astype(jnp.int32) + has_prev.astype(jnp.int32))

    def remote(src, dst, sems, i, device):
        return pltpu.make_async_remote_copy(
            src_ref=src,
            dst_ref=dst,
            send_sem=sems.at[0, i],
            recv_sem=sems.at[1, i],
            device_id={"tm": device},
            device_id_type=MESH,
        )

    def same(ref, sems, i, device):
        return remote(ref, ref, sems, i, device)

    def rows_at(chunk):
        return pl.ds(pl.multiple_of(chunk * unit, unit), unit)

    group = order // QUAD

    def to_core(owner, g):
        return same(local2.at[owner, pl.ds(g * group, group)], core_sem, g, core_mate)

    for g in range(QUAD):
        to_core(core, g).start()

    @pl.when(core == 0)
    def _():
        for g in range(QUAD):
            to_core(1 - core, g).wait_recv()

    high, low = halves(local2[1])
    right_high[...] = high
    right_low[...] = low

    def x_copy(side, c, j):
        return same(chip2.at[side, rows_at(2 * j + c)], x_sem, j, x_mate)

    def x_forward(c, j):
        return same(chip2.at[1 - x, rows_at(2 * j + c)], xf_sem, j, core_mate)

    for g in range(QUAD):

        @pl.when(core == 1)
        def _():
            to_core(1 - core, g).wait_recv()

        rows = slice(g * group, (g + 1) * group)
        chip2[x, rows] = times(local2[0, rows], local2[1, rows], right_high[...], right_low[...])

        @pl.when(sends_x)
        def _():
            for j in range(g * per_core // QUAD, (g + 1) * per_core // QUAD):
                x_copy(x, core, j).start()

    def make_release():
        fetches[1].wait()
        fetches[2].wait()
        ids = batch[...]
        column_scale = jnp.zeros(ids.shape, jnp.float32)
        for b in range(amplitude.shape[0]):
            column_scale = jnp.where(ids == b, amplitude[b], column_scale)
        release[...] = (coeffs[...].astype(jnp.float32) * column_scale).astype(jnp.bfloat16)
        store.start()

    pl.when(has_prev)(make_release)

    def send_back(s):
        here = pl.ds(pl.multiple_of(s * unit, unit), unit)
        return remote(back.at[here], sent.at[here], back_sem, s, x_mate)

    def chain(c_lane, s):
        here = pl.ds(pl.multiple_of(s * unit, unit), unit)
        chunk = (c_lane // 2) * per_core + 2 * s + c_lane % 2
        return remote(sent.at[here], reach_in.at[rows_at(chunk)], z_sem, s, me + QUAD)

    @pl.when(jnp.logical_and(first, x == 1))
    def _():
        high, low = halves(chip2[1])
        right_high[...] = high
        right_low[...] = low

        def step(j):
            x_copy(1 - x, core, j).wait_recv()
            x_forward(core, j).start()
            rows = rows_at(2 * j + core)
            return times(chip2[0, rows], chip2[1, rows], right_high[...], right_low[...])

        @pl.loop(0, per_lane)
        def _(j):
            back[pl.ds(pl.multiple_of(j * unit, unit), unit)] = step(j)
            send_back(j).start()

        @pl.loop(0, per_lane)
        def _(s):
            sent[pl.ds(pl.multiple_of(s * unit, unit), unit)] = step(s + per_lane)

            @pl.when(has_next)
            def _():
                chain(lane, s).start()

    @pl.when(jnp.logical_and(first, x == 0))
    def _():
        @pl.loop(0, per_lane)
        def _(s):
            send_back(s).wait_recv()

            @pl.when(has_next)
            def _():
                chain(lane, s).start()

    def split_quad():
        high, low = halves(quad[...])
        quad_high[...] = high
        quad_low[...] = low

    @pl.when(has_prev)
    def _():
        high, low = halves(chip2[x])
        right_high[...] = high
        right_low[...] = low
        per_group = per_core // QUAD

        @pl.when(x == 0)
        def _():
            quad[...] = chip2[0]

        def add_group(g):
            for j in range(g * per_group, (g + 1) * per_group):
                x_forward(1 - core, j).wait_recv()
            rows = slice(g * group, (g + 1) * group)

            @pl.when(x == 1)
            def _():
                quad[rows] = times(
                    chip2[0, rows], chip2[1, rows], right_high[...], right_low[...]
                )

            @pl.when(x == 0)
            def _():
                high, low = halves(chip2[1, rows])
                left_high, left_low = right_high[:, rows], right_low[:, rows]
                quad[...] += mul(left_high, high) + (mul(left_high, low) + mul(left_low, high))
                quad[rows] += chip2[1, rows]

        for g in range(QUAD):

            @pl.loop(g * per_group, (g + 1) * per_group)
            def _(j):
                x_copy(1 - x, core, j).wait_recv()
                x_forward(core, j).start()

            if g:
                add_group(g - 1)
        add_group(QUAD - 1)
        split_quad()

    pl.when(first)(make_release)

    @pl.when(jnp.logical_and(first, x == 1))
    def _():
        @pl.loop(0, per_core)
        def _(j):
            x_forward(1 - core, j).wait_recv()

        quad[...] = times(chip2[0], chip2[1], right_high[...], right_low[...])

    def make_within():
        @pl.when(lane == 0)
        def _():
            within[...] = local2[0]

        @pl.when(lane == 1)
        def _():
            within[...] = chip2[0]

        @pl.when(lane == 2)
        def _():
            high, low = halves(local2[0])
            within[...] = times(chip2[0], local2[0], high, low)

        @pl.when(lane == 3)
        def _():
            within[...] = quad[...]

        high, low = halves(within[...])
        right_high[...] = high
        right_low[...] = low

    pl.when(jnp.logical_not(has_next))(make_within)

    def lane_rows(c_lane, s):
        return rows_at((c_lane // 2) * per_core + 2 * s + c_lane % 2)

    def shared(sems, c_lane, device, s):
        return same(reach_in.at[lane_rows(c_lane, s)], sems, s, device)

    x_lane = lane + 2 - 4 * x
    core_lane = lane + 1 - 2 * core
    xc_lane = x_lane + 1 - 2 * core

    def share_x(s):
        shared(ex_sem, x_lane, x_mate, s).wait_recv()
        shared(exf_sem, x_lane, core_mate, s).start()

    @pl.when(has_prev)
    def _():
        @pl.loop(0, per_lane)
        def _(s):
            chain(lane, s).wait_recv()
            shared(ex_sem, lane, x_mate, s).start()
            shared(ef_sem, lane, core_mate, s).start()

            @pl.when(has_next)
            def _():
                rows = lane_rows(lane, s)
                sent[pl.ds(pl.multiple_of(s * unit, unit), unit)] = times(
                    reach_in[rows], quad[rows], quad_high[...], quad_low[...]
                )
                chain(lane, s).start()

            @pl.when(s > 1)
            def _():
                share_x(s - 2)

    pl.when(has_next)(make_within)

    def finish(value, start, size):
        shape = (size, order)
        diagonal = start + lax.broadcasted_iota(
            jnp.int32, shape, 0
        ) == lax.broadcasted_iota(jnp.int32, shape, 1)
        value = value + jnp.where(diagonal, jnp.float32(1.0), jnp.float32(0.0))
        reach_out[:, pl.ds(start, size)] = value.T.astype(jnp.bfloat16)

    @pl.when(first)
    def _():
        finish(within[...], 0, order)

    half = order // 2

    def finish_half(side):
        start = pl.multiple_of(side * half, half)
        rows = pl.ds(start, half)
        finish(
            times(reach_in[rows], within[rows], right_high[...], right_low[...]), start, half
        )

    @pl.when(has_prev)
    def _():
        share_x(per_lane - 2)
        share_x(per_lane - 1)

        @pl.loop(0, per_lane)
        def _(s):
            shared(ef_sem, core_lane, core_mate, s).wait_recv()

        finish_half(x)

        @pl.loop(0, per_lane)
        def _(s):
            shared(exf_sem, xc_lane, core_mate, s).wait_recv()

        finish_half(1 - x)

    store.wait()
    for g in range(QUAD):
        to_core(core, g).wait_send()

    @pl.when(sends_x)
    def _():
        @pl.loop(0, per_core)
        def _(j):
            x_copy(x, core, j).wait_send()

    @pl.when(gets_x)
    def _():
        @pl.loop(0, per_core)
        def _(j):
            x_forward(core, j).wait_send()

    @pl.when(jnp.logical_and(first, x == 1))
    def _():
        @pl.loop(0, per_lane)
        def _(s):
            send_back(s).wait_send()

    @pl.when(has_next)
    def _():
        @pl.loop(0, per_lane)
        def _(s):
            chain(lane, s).wait_send()

    @pl.when(has_prev)
    def _():
        @pl.loop(0, per_lane)
        def _(s):
            shared(ex_sem, lane, x_mate, s).wait_send()
            shared(ef_sem, lane, core_mate, s).wait_send()
            shared(exf_sem, x_lane, core_mate, s).wait_send()


def on_device(
    count, perturbation, hours_live, start_hour, release_coeffs, batch_of_column, batch_amplitude
):
    order = perturbation.shape[1]
    columns = release_coeffs.shape[1]
    vmem = pl.BlockSpec(memory_space=pltpu.VMEM)
    smem = pl.BlockSpec(memory_space=pltpu.SMEM)
    anywhere = pl.BlockSpec(memory_space=pl.ANY)
    f32, bf16 = jnp.float32, jnp.bfloat16
    square = (order, order)
    sems = lambda n: pltpu.SemaphoreType.DMA((2, n))
    reach, release = pl.pallas_call(
        functools.partial(kernel, count),
        out_shape=(
            jax.ShapeDtypeStruct(square, bf16),
            jax.ShapeDtypeStruct((order, columns), bf16),
        ),
        in_specs=[smem, smem, smem, anywhere, anywhere, anywhere],
        out_specs=(vmem, anywhere),
        scratch_shapes=[
            pltpu.VMEM((order, columns), bf16),
            pltpu.VMEM(perturbation.shape, bf16),
            pltpu.VMEM((order, columns), bf16),
            pltpu.VMEM((1, columns), jnp.int32),
            pltpu.VMEM((2,) + square, f32),
            pltpu.VMEM((2,) + square, f32),
            pltpu.VMEM(square, f32),
            pltpu.VMEM(square, f32),
            pltpu.VMEM(square, f32),
            pltpu.VMEM((order // QUAD, order), f32),
            pltpu.VMEM((order // QUAD, order), f32),
            pltpu.VMEM(square, bf16),
            pltpu.VMEM(square, bf16),
            pltpu.VMEM(square, bf16),
            pltpu.VMEM(square, bf16),
            pltpu.SemaphoreType.DMA((4,)),
            sems(QUAD),
            sems(UNITS // 2),
            sems(UNITS // 2),
            sems(UNITS // QUAD),
            sems(UNITS // QUAD),
            sems(UNITS // QUAD),
            sems(UNITS // QUAD),
            sems(UNITS // QUAD),
        ],
        compiler_params=pltpu.CompilerParams(
            collective_id=0, has_side_effects=True, vmem_limit_bytes=60 * 1024 * 1024
        ),
    )(
        hours_live,
        start_hour,
        batch_amplitude,
        perturbation,
        release_coeffs,
        batch_of_column[None, :],
    )
    panel = jnp.dot(reach, release, preferred_element_type=jnp.float32)
    return panel.astype(bf16)[None, :, :]


def solution(mesh):
    in_specs = (
        P(("basin", "tm"), None, None),
        P(("basin", "tm")),
        P(),
        P("basin", None),
        P("basin"),
        P("basin"),
    )
    out_specs = P(("basin", "tm"), None, None)
    return jax.shard_map(
        functools.partial(on_device, mesh.shape["tm"]),
        mesh=mesh,
        in_specs=in_specs,
        out_specs=out_specs,
        check_vma=False,
    )
```

```python
import functools
import jax
import jax.numpy as jnp
from jax import lax
from jax.experimental import pallas as pl
from jax.experimental.pallas import tpu as pltpu
from jax.sharding import PartitionSpec as P

MESH = pl.DeviceIdType.MESH
QUAD = 4
UNITS = 32
LAG = 4


def halves(value):
    high = value.astype(jnp.bfloat16)
    return high, (value - high.astype(jnp.float32)).astype(jnp.bfloat16)


def mul(a, b):
    return jnp.dot(a, b, preferred_element_type=jnp.float32)


def times(left, right, right_high, right_low):
    high, low = halves(left)
    return left + right + (mul(high, right_high) + (mul(high, right_low) + mul(low, right_high)))


def kernel(
    count,
    hours_live,
    start_hour,
    amplitude_in,
    pert_in,
    coeffs_in,
    batch_in,
    reach_out,
    release,
    amplitude,
    pert,
    coeffs,
    batch,
    local2,
    chip2,
    quad,
    reach_in,
    within,
    sent,
    back,
    right_high,
    right_low,
    quad_high,
    quad_low,
    in_sem,
    core_sem,
    x_sem,
    xf_sem,
    back_sem,
    z_sem,
    ef_sem,
    ex_sem,
    exf_sem,
):
    order = pert.shape[1]
    unit = order // UNITS
    per_core = UNITS // 2
    per_lane = UNITS // QUAD
    me = lax.axis_index("tm")
    core = me % 2
    x = (me // 2) % 2
    lane = me % QUAD
    q = me // QUAD
    core_mate = me + 1 - 2 * core
    x_mate = me + 2 - 4 * x
    has_next = q < count // QUAD - 1
    has_prev = q > 0
    first = q == 0
    gets_x = jnp.logical_or(has_prev, x == 1)
    sends_x = jnp.logical_or(has_prev, x == 0)

    fetches = [
        pltpu.make_async_copy(src, dst, in_sem.at[i])
        for i, (src, dst) in enumerate(
            (
                (pert_in, pert),
                (coeffs_in, coeffs),
                (batch_in, batch),
                (amplitude_in, amplitude),
            )
        )
    ]
    for fetch in fetches:
        fetch.start()
    barrier = pltpu.get_barrier_semaphore()
    for mate in (core_mate, x_mate):
        pl.semaphore_signal(barrier, inc=1, device_id={"tm": mate}, device_id_type=MESH)

    @pl.when(has_next)
    def _():
        pl.semaphore_signal(barrier, inc=1, device_id={"tm": me + QUAD}, device_id_type=MESH)

    @pl.when(has_prev)
    def _():
        pl.semaphore_signal(barrier, inc=1, device_id={"tm": me - QUAD}, device_id_type=MESH)

    scales = []
    for j in range(pert.shape[0]):
        alive = jnp.logical_and(j < hours_live[0], me * pert.shape[0] + j >= start_hour[0])
        scales.append(jnp.where(alive, jnp.float32(1.0), jnp.float32(0.0)))
    fetches[0].wait()
    total = pert[0].astype(jnp.float32) * scales[0]
    for j in range(1, pert.shape[0]):
        left = pert[j].astype(jnp.float32) * scales[j]
        high, low = halves(total)
        factor = left.astype(jnp.bfloat16)
        product = mul(factor, high)
        if j > 1:
            product = product + mul(factor, low)
        total = total + left + product
    local2[core] = total.T

    pl.semaphore_wait(barrier, 2 + has_next.astype(jnp.int32) + has_prev.astype(jnp.int32))

    def remote(src, dst, sems, i, device):
        return pltpu.make_async_remote_copy(
            src_ref=src,
            dst_ref=dst,
            send_sem=sems.at[0, i],
            recv_sem=sems.at[1, i],
            device_id={"tm": device},
            device_id_type=MESH,
        )

    def same(ref, sems, i, device):
        return remote(ref, ref, sems, i, device)

    def rows_at(chunk):
        return pl.ds(pl.multiple_of(chunk * unit, unit), unit)

    group = order // QUAD

    def to_core(owner, g):
        return same(local2.at[owner, pl.ds(g * group, group)], core_sem, g, core_mate)

    for g in range(QUAD):
        to_core(core, g).start()

    @pl.when(core == 0)
    def _():
        for g in range(QUAD):
            to_core(1 - core, g).wait_recv()

    high, low = halves(local2[1])
    right_high[...] = high
    right_low[...] = low

    def x_copy(side, c, j):
        return same(chip2.at[side, rows_at(2 * j + c)], x_sem, j, x_mate)

    def x_forward(c, j):
        return same(chip2.at[1 - x, rows_at(2 * j + c)], xf_sem, j, core_mate)

    for g in range(QUAD):

        @pl.when(core == 1)
        def _():
            to_core(1 - core, g).wait_recv()

        rows = slice(g * group, (g + 1) * group)
        chip2[x, rows] = times(local2[0, rows], local2[1, rows], right_high[...], right_low[...])

        @pl.when(sends_x)
        def _():
            for j in range(g * per_core // QUAD, (g + 1) * per_core // QUAD):
                x_copy(x, core, j).start()

    def make_release():
        for fetch in fetches[1:]:
            fetch.wait()
        ids = batch[...]
        column_scale = jnp.zeros(ids.shape, jnp.float32)
        for b in range(amplitude.shape[0]):
            column_scale = jnp.where(ids == b, amplitude[b], column_scale)
        release[...] = (coeffs[...].astype(jnp.float32) * column_scale).astype(jnp.bfloat16)

    pl.when(has_prev)(make_release)

    def send_back(s):
        here = pl.ds(pl.multiple_of(s * unit, unit), unit)
        return remote(back.at[here], sent.at[here], back_sem, s, x_mate)

    def chain(c_lane, s):
        here = pl.ds(pl.multiple_of(s * unit, unit), unit)
        chunk = (c_lane // 2) * per_core + 2 * s + c_lane % 2
        return remote(sent.at[here], reach_in.at[rows_at(chunk)], z_sem, s, me + QUAD)

    @pl.when(jnp.logical_and(first, x == 1))
    def _():
        high, low = halves(chip2[1])
        right_high[...] = high
        right_low[...] = low

        def step(j):
            x_copy(1 - x, core, j).wait_recv()
            x_forward(core, j).start()
            rows = rows_at(2 * j + core)
            return times(chip2[0, rows], chip2[1, rows], right_high[...], right_low[...])

        @pl.loop(0, per_lane)
        def _(j):
            back[pl.ds(pl.multiple_of(j * unit, unit), unit)] = step(j)
            send_back(j).start()

        @pl.loop(0, per_lane)
        def _(s):
            sent[pl.ds(pl.multiple_of(s * unit, unit), unit)] = step(s + per_lane)

            @pl.when(has_next)
            def _():
                chain(lane, s).start()

    @pl.when(jnp.logical_and(first, x == 0))
    def _():
        @pl.loop(0, per_lane)
        def _(s):
            send_back(s).wait_recv()

            @pl.when(has_next)
            def _():
                chain(lane, s).start()

    def split_quad():
        high, low = halves(quad[...])
        quad_high[...] = high
        quad_low[...] = low

    @pl.when(has_prev)
    def _():
        high, low = halves(chip2[x])
        right_high[...] = high
        right_low[...] = low
        per_group = per_core // QUAD

        @pl.when(x == 0)
        def _():
            quad[...] = chip2[0]

        def add_group(g):
            for j in range(g * per_group, (g + 1) * per_group):
                x_forward(1 - core, j).wait_recv()
            rows = slice(g * group, (g + 1) * group)

            @pl.when(x == 1)
            def _():
                quad[rows] = times(
                    chip2[0, rows], chip2[1, rows], right_high[...], right_low[...]
                )

            @pl.when(x == 0)
            def _():
                high, low = halves(chip2[1, rows])
                left_high, left_low = right_high[:, rows], right_low[:, rows]
                quad[...] += mul(left_high, high) + (mul(left_high, low) + mul(left_low, high))
                quad[rows] += chip2[1, rows]

        def pass_on(start, stop):
            @pl.loop(start, stop)
            def _(j):
                x_copy(1 - x, core, j).wait_recv()
                x_forward(core, j).start()

        ahead = per_group // 2
        pass_on(0, per_group + ahead)
        for g in range(QUAD - 1):
            add_group(g)
            pass_on((g + 1) * per_group + ahead, min((g + 2) * per_group + ahead, per_core))
        add_group(QUAD - 1)
        split_quad()

    pl.when(first)(make_release)

    @pl.when(jnp.logical_and(first, x == 1))
    def _():
        @pl.loop(0, per_core)
        def _(j):
            x_forward(1 - core, j).wait_recv()

        quad[...] = times(chip2[0], chip2[1], right_high[...], right_low[...])

    def make_within():
        @pl.when(lane == 0)
        def _():
            within[...] = local2[0]

        @pl.when(lane == 1)
        def _():
            within[...] = chip2[0]

        @pl.when(lane == 2)
        def _():
            high, low = halves(local2[0])
            within[...] = times(chip2[0], local2[0], high, low)

        @pl.when(lane == 3)
        def _():
            within[...] = quad[...]

        high, low = halves(within[...])
        right_high[...] = high
        right_low[...] = low

    pl.when(jnp.logical_not(has_next))(make_within)

    def lane_rows(c_lane, s):
        return rows_at((c_lane // 2) * per_core + 2 * s + c_lane % 2)

    def shared(sems, c_lane, device, s):
        return same(reach_in.at[lane_rows(c_lane, s)], sems, s, device)

    x_lane = lane + 2 - 4 * x
    core_lane = lane + 1 - 2 * core
    xc_lane = x_lane + 1 - 2 * core

    def share_x(s):
        shared(ex_sem, x_lane, x_mate, s).wait_recv()
        shared(exf_sem, x_lane, core_mate, s).start()

    @pl.when(has_prev)
    def _():
        @pl.loop(0, per_lane)
        def _(s):
            chain(lane, s).wait_recv()
            shared(ex_sem, lane, x_mate, s).start()
            shared(ef_sem, lane, core_mate, s).start()

            @pl.when(has_next)
            def _():
                rows = lane_rows(lane, s)
                sent[pl.ds(pl.multiple_of(s * unit, unit), unit)] = times(
                    reach_in[rows], quad[rows], quad_high[...], quad_low[...]
                )
                chain(lane, s).start()

            @pl.when(s >= LAG)
            def _():
                share_x(s - LAG)

    pl.when(has_next)(make_within)

    def finish(value, start, size):
        shape = (size, order)
        diagonal = start + lax.broadcasted_iota(
            jnp.int32, shape, 0
        ) == lax.broadcasted_iota(jnp.int32, shape, 1)
        value = value + jnp.where(diagonal, jnp.float32(1.0), jnp.float32(0.0))
        reach_out[:, pl.ds(start, size)] = value.T.astype(jnp.bfloat16)

    @pl.when(first)
    def _():
        finish(within[...], 0, order)

    half = order // 2

    def finish_half(side):
        start = pl.multiple_of(side * half, half)
        rows = pl.ds(start, half)
        finish(
            times(reach_in[rows], within[rows], right_high[...], right_low[...]), start, half
        )

    @pl.when(has_prev)
    def _():
        for s in range(per_lane - LAG, per_lane):
            share_x(s)

        @pl.loop(0, per_lane)
        def _(s):
            shared(ef_sem, core_lane, core_mate, s).wait_recv()

        finish_half(x)

        @pl.loop(0, per_lane)
        def _(s):
            shared(exf_sem, xc_lane, core_mate, s).wait_recv()

        finish_half(1 - x)

    for g in range(QUAD):
        to_core(core, g).wait_send()

    @pl.when(sends_x)
    def _():
        @pl.loop(0, per_core)
        def _(j):
            x_copy(x, core, j).wait_send()

    @pl.when(gets_x)
    def _():
        @pl.loop(0, per_core)
        def _(j):
            x_forward(core, j).wait_send()

    @pl.when(jnp.logical_and(first, x == 1))
    def _():
        @pl.loop(0, per_lane)
        def _(s):
            send_back(s).wait_send()

    @pl.when(has_next)
    def _():
        @pl.loop(0, per_lane)
        def _(s):
            chain(lane, s).wait_send()

    @pl.when(has_prev)
    def _():
        @pl.loop(0, per_lane)
        def _(s):
            shared(ex_sem, lane, x_mate, s).wait_send()
            shared(ef_sem, lane, core_mate, s).wait_send()
            shared(exf_sem, x_lane, core_mate, s).wait_send()


def on_device(
    count, perturbation, hours_live, start_hour, release_coeffs, batch_of_column, batch_amplitude
):
    order = perturbation.shape[1]
    columns = release_coeffs.shape[1]
    vmem = pl.BlockSpec(memory_space=pltpu.VMEM)
    smem = pl.BlockSpec(memory_space=pltpu.SMEM)
    hbm = pl.BlockSpec(memory_space=pltpu.HBM)
    f32, bf16 = jnp.float32, jnp.bfloat16
    square = (order, order)
    sems = lambda n: pltpu.SemaphoreType.DMA((2, n))
    reach, release = pl.pallas_call(
        functools.partial(kernel, count),
        out_shape=(
            jax.ShapeDtypeStruct(square, bf16),
            jax.ShapeDtypeStruct((order, columns), bf16),
        ),
        in_specs=[smem, smem, hbm, hbm, hbm, hbm],
        out_specs=(vmem, vmem),
        scratch_shapes=[
            pltpu.SMEM(batch_amplitude.shape, f32),
            pltpu.VMEM(perturbation.shape, bf16),
            pltpu.VMEM((order, columns), bf16),
            pltpu.VMEM((1, columns), jnp.int32),
            pltpu.VMEM((2,) + square, f32),
            pltpu.VMEM((2,) + square, f32),
            pltpu.VMEM(square, f32),
            pltpu.VMEM(square, f32),
            pltpu.VMEM(square, f32),
            pltpu.VMEM((order // QUAD, order), f32),
            pltpu.VMEM((order // QUAD, order), f32),
            pltpu.VMEM(square, bf16),
            pltpu.VMEM(square, bf16),
            pltpu.VMEM(square, bf16),
            pltpu.VMEM(square, bf16),
            pltpu.SemaphoreType.DMA((4,)),
            sems(QUAD),
            sems(UNITS // 2),
            sems(UNITS // 2),
            sems(UNITS // QUAD),
            sems(UNITS // QUAD),
            sems(UNITS // QUAD),
            sems(UNITS // QUAD),
            sems(UNITS // QUAD),
        ],
        compiler_params=pltpu.CompilerParams(
            collective_id=0, has_side_effects=True, vmem_limit_bytes=40 * 1024 * 1024
        ),
    )(
        hours_live,
        start_hour,
        *(
            pltpu.with_memory_space_constraint(value, pltpu.HBM)
            for value in (batch_amplitude, perturbation, release_coeffs, batch_of_column[None, :])
        ),
    )
    panel = jnp.dot(reach, release, preferred_element_type=jnp.float32)
    return panel.astype(bf16)[None, :, :]


def solution(mesh):
    in_specs = (
        P(("basin", "tm"), None, None),
        P(("basin", "tm")),
        P(),
        P("basin", None),
        P("basin"),
        P("basin"),
    )
    out_specs = P(("basin", "tm"), None, None)
    return jax.shard_map(
        functools.partial(on_device, mesh.shape["tm"]),
        mesh=mesh,
        in_specs=in_specs,
        out_specs=out_specs,
        check_vma=False,
    )
```

```python
import functools
import jax
import jax.numpy as jnp
from jax import lax
from jax.experimental import pallas as pl
from jax.experimental.pallas import tpu as pltpu
from jax.sharding import PartitionSpec as P

MESH = pl.DeviceIdType.MESH
QUAD = 4
UNITS = 32
LAG = 4


def halves(value):
    high = value.astype(jnp.bfloat16)
    return high, (value - high.astype(jnp.float32)).astype(jnp.bfloat16)


def mul(a, b):
    return jnp.dot(a, b, preferred_element_type=jnp.float32)


def times(left, right, right_high, right_low):
    high, low = halves(left)
    rows = left.shape[0]
    both = mul(jnp.concatenate([high, low], axis=0), right_high)
    return left + right + (both[:rows] + (mul(high, right_low) + both[rows:]))


def kernel(
    count,
    hours_live,
    start_hour,
    amplitude_in,
    pert_in,
    coeffs_in,
    batch_in,
    reach_out,
    release,
    amplitude,
    pert,
    coeffs,
    batch,
    local2,
    chip2,
    quad,
    reach_in,
    within,
    sent,
    back,
    right_high,
    right_low,
    quad_high,
    quad_low,
    in_sem,
    core_sem,
    x_sem,
    xf_sem,
    back_sem,
    z_sem,
    ef_sem,
    ex_sem,
    exf_sem,
):
    order = pert.shape[1]
    unit = order // UNITS
    per_core = UNITS // 2
    per_lane = UNITS // QUAD
    me = lax.axis_index("tm")
    core = me % 2
    x = (me // 2) % 2
    lane = me % QUAD
    q = me // QUAD
    core_mate = me + 1 - 2 * core
    x_mate = me + 2 - 4 * x
    has_next = q < count // QUAD - 1
    has_prev = q > 0
    first = q == 0
    gets_x = jnp.logical_or(has_prev, x == 1)
    sends_x = jnp.logical_or(has_prev, x == 0)

    fetches = [
        pltpu.make_async_copy(src, dst, in_sem.at[i])
        for i, (src, dst) in enumerate(
            (
                (pert_in, pert),
                (coeffs_in, coeffs),
                (batch_in, batch),
                (amplitude_in, amplitude),
            )
        )
    ]
    for fetch in fetches:
        fetch.start()
    barrier = pltpu.get_barrier_semaphore()
    for mate in (core_mate, x_mate):
        pl.semaphore_signal(barrier, inc=1, device_id={"tm": mate}, device_id_type=MESH)

    @pl.when(has_next)
    def _():
        pl.semaphore_signal(barrier, inc=1, device_id={"tm": me + QUAD}, device_id_type=MESH)

    @pl.when(has_prev)
    def _():
        pl.semaphore_signal(barrier, inc=1, device_id={"tm": me - QUAD}, device_id_type=MESH)

    scales = []
    for j in range(pert.shape[0]):
        alive = jnp.logical_and(j < hours_live[0], me * pert.shape[0] + j >= start_hour[0])
        scales.append(jnp.where(alive, jnp.float32(1.0), jnp.float32(0.0)))
    fetches[0].wait()
    total = pert[0].astype(jnp.float32) * scales[0]
    for j in range(1, pert.shape[0]):
        left = pert[j].astype(jnp.float32) * scales[j]
        high, low = halves(total)
        factor = left.astype(jnp.bfloat16)
        product = mul(factor, high)
        if j > 1:
            product = product + mul(factor, low)
        total = total + left + product
    local2[core] = total.T

    pl.semaphore_wait(barrier, 2 + has_next.astype(jnp.int32) + has_prev.astype(jnp.int32))

    def remote(src, dst, sems, i, device):
        return pltpu.make_async_remote_copy(
            src_ref=src,
            dst_ref=dst,
            send_sem=sems.at[0, i],
            recv_sem=sems.at[1, i],
            device_id={"tm": device},
            device_id_type=MESH,
        )

    def same(ref, sems, i, device):
        return remote(ref, ref, sems, i, device)

    def rows_at(chunk):
        return pl.ds(pl.multiple_of(chunk * unit, unit), unit)

    group = order // QUAD

    def to_core(owner, g):
        return same(local2.at[owner, pl.ds(g * group, group)], core_sem, g, core_mate)

    for g in range(QUAD):
        to_core(core, g).start()

    @pl.when(core == 0)
    def _():
        for g in range(QUAD):
            to_core(1 - core, g).wait_recv()

    high, low = halves(local2[1])
    right_high[...] = high
    right_low[...] = low

    def x_copy(side, c, j):
        return same(chip2.at[side, rows_at(2 * j + c)], x_sem, j, x_mate)

    def x_forward(c, j):
        return same(chip2.at[1 - x, rows_at(2 * j + c)], xf_sem, j, core_mate)

    for g in range(QUAD):

        @pl.when(core == 1)
        def _():
            to_core(1 - core, g).wait_recv()

        rows = slice(g * group, (g + 1) * group)
        chip2[x, rows] = times(local2[0, rows], local2[1, rows], right_high[...], right_low[...])

        @pl.when(sends_x)
        def _():
            for j in range(g * per_core // QUAD, (g + 1) * per_core // QUAD):
                x_copy(x, core, j).start()

    def make_release():
        for fetch in fetches[1:]:
            fetch.wait()
        ids = batch[...]
        column_scale = jnp.zeros(ids.shape, jnp.float32)
        for b in range(amplitude.shape[0]):
            column_scale = jnp.where(ids == b, amplitude[b], column_scale)
        release[...] = (coeffs[...].astype(jnp.float32) * column_scale).astype(jnp.bfloat16)

    pl.when(has_prev)(make_release)

    def send_back(s):
        here = pl.ds(pl.multiple_of(s * unit, unit), unit)
        return remote(back.at[here], sent.at[here], back_sem, s, x_mate)

    def chain(c_lane, s):
        here = pl.ds(pl.multiple_of(s * unit, unit), unit)
        chunk = (c_lane // 2) * per_core + 2 * s + c_lane % 2
        return remote(sent.at[here], reach_in.at[rows_at(chunk)], z_sem, s, me + QUAD)

    @pl.when(jnp.logical_and(first, x == 1))
    def _():
        high, low = halves(chip2[1])
        right_high[...] = high
        right_low[...] = low

        def step(j):
            x_copy(1 - x, core, j).wait_recv()
            x_forward(core, j).start()
            rows = rows_at(2 * j + core)
            return times(chip2[0, rows], chip2[1, rows], right_high[...], right_low[...])

        @pl.loop(0, per_lane)
        def _(j):
            back[pl.ds(pl.multiple_of(j * unit, unit), unit)] = step(j)
            send_back(j).start()

        @pl.loop(0, per_lane)
        def _(s):
            sent[pl.ds(pl.multiple_of(s * unit, unit), unit)] = step(s + per_lane)

            @pl.when(has_next)
            def _():
                chain(lane, s).start()

    @pl.when(jnp.logical_and(first, x == 0))
    def _():
        @pl.loop(0, per_lane)
        def _(s):
            send_back(s).wait_recv()

            @pl.when(has_next)
            def _():
                chain(lane, s).start()

    def split_quad():
        high, low = halves(quad[...])
        quad_high[...] = high
        quad_low[...] = low

    @pl.when(has_prev)
    def _():
        high, low = halves(chip2[x])
        right_high[...] = high
        right_low[...] = low
        per_group = per_core // QUAD

        @pl.when(x == 0)
        def _():
            quad[...] = chip2[0]

        def add_group(g):
            for j in range(g * per_group, (g + 1) * per_group):
                x_forward(1 - core, j).wait_recv()
            rows = slice(g * group, (g + 1) * group)

            @pl.when(x == 1)
            def _():
                quad[rows] = times(
                    chip2[0, rows], chip2[1, rows], right_high[...], right_low[...]
                )

            @pl.when(x == 0)
            def _():
                high, low = halves(chip2[1, rows])
                left_high, left_low = right_high[:, rows], right_low[:, rows]
                quad[...] += mul(left_high, high) + (mul(left_high, low) + mul(left_low, high))
                quad[rows] += chip2[1, rows]

        def pass_on(start, stop):
            @pl.loop(start, stop)
            def _(j):
                x_copy(1 - x, core, j).wait_recv()
                x_forward(core, j).start()

        ahead = per_group // 2
        pass_on(0, per_group + ahead)
        for g in range(QUAD - 1):
            add_group(g)
            pass_on((g + 1) * per_group + ahead, min((g + 2) * per_group + ahead, per_core))
        add_group(QUAD - 1)
        split_quad()

    pl.when(first)(make_release)

    @pl.when(jnp.logical_and(first, x == 1))
    def _():
        @pl.loop(0, per_core)
        def _(j):
            x_forward(1 - core, j).wait_recv()

        quad[...] = times(chip2[0], chip2[1], right_high[...], right_low[...])

    def make_within():
        @pl.when(lane == 0)
        def _():
            within[...] = local2[0]

        @pl.when(lane == 1)
        def _():
            within[...] = chip2[0]

        @pl.when(lane == 2)
        def _():
            high, low = halves(local2[0])
            within[...] = times(chip2[0], local2[0], high, low)

        @pl.when(lane == 3)
        def _():
            within[...] = quad[...]

        high, low = halves(within[...])
        right_high[...] = high
        right_low[...] = low

    pl.when(jnp.logical_not(has_next))(make_within)

    def lane_rows(c_lane, s):
        return rows_at((c_lane // 2) * per_core + 2 * s + c_lane % 2)

    def shared(sems, c_lane, device, s):
        return same(reach_in.at[lane_rows(c_lane, s)], sems, s, device)

    x_lane = lane + 2 - 4 * x
    core_lane = lane + 1 - 2 * core
    xc_lane = x_lane + 1 - 2 * core

    def share_x(s):
        shared(ex_sem, x_lane, x_mate, s).wait_recv()
        shared(exf_sem, x_lane, core_mate, s).start()

    @pl.when(has_prev)
    def _():
        @pl.loop(0, per_lane)
        def _(s):
            chain(lane, s).wait_recv()

            @pl.when(has_next)
            def _():
                rows = lane_rows(lane, s)
                sent[pl.ds(pl.multiple_of(s * unit, unit), unit)] = times(
                    reach_in[rows], quad[rows], quad_high[...], quad_low[...]
                )
                chain(lane, s).start()

            shared(ex_sem, lane, x_mate, s).start()
            shared(ef_sem, lane, core_mate, s).start()

            @pl.when(s >= LAG)
            def _():
                share_x(s - LAG)

    pl.when(has_next)(make_within)

    def finish(value, start, size):
        shape = (size, order)
        diagonal = start + lax.broadcasted_iota(
            jnp.int32, shape, 0
        ) == lax.broadcasted_iota(jnp.int32, shape, 1)
        value = value + jnp.where(diagonal, jnp.float32(1.0), jnp.float32(0.0))
        reach_out[:, pl.ds(start, size)] = value.T.astype(jnp.bfloat16)

    @pl.when(first)
    def _():
        finish(within[...], 0, order)

    half = order // 2

    def finish_half(side):
        start = pl.multiple_of(side * half, half)
        rows = pl.ds(start, half)
        finish(
            times(reach_in[rows], within[rows], right_high[...], right_low[...]), start, half
        )

    def drain():
        for g in range(QUAD):
            to_core(core, g).wait_send()

        @pl.when(sends_x)
        def _():
            @pl.loop(0, per_core)
            def _(j):
                x_copy(x, core, j).wait_send()

        @pl.when(gets_x)
        def _():
            @pl.loop(0, per_core)
            def _(j):
                x_forward(core, j).wait_send()

        @pl.when(jnp.logical_and(first, x == 1))
        def _():
            @pl.loop(0, per_lane)
            def _(s):
                send_back(s).wait_send()

    @pl.when(has_prev)
    def _():
        for s in range(per_lane - LAG, per_lane - 2):
            share_x(s)

        @pl.loop(0, per_lane)
        def _(s):
            shared(ef_sem, core_lane, core_mate, s).wait_recv()

        finish_half(x)
        for s in range(per_lane - 2, per_lane):
            share_x(s)
        drain()

        @pl.loop(0, per_lane)
        def _(s):
            shared(exf_sem, xc_lane, core_mate, s).wait_recv()

        finish_half(1 - x)

    pl.when(first)(drain)

    @pl.when(has_next)
    def _():
        @pl.loop(0, per_lane)
        def _(s):
            chain(lane, s).wait_send()

    @pl.when(has_prev)
    def _():
        @pl.loop(0, per_lane)
        def _(s):
            shared(ex_sem, lane, x_mate, s).wait_send()
            shared(ef_sem, lane, core_mate, s).wait_send()
            shared(exf_sem, x_lane, core_mate, s).wait_send()


def panel_tile(reach, release, panel):
    panel[0] = mul(reach[...], release[...]).astype(panel.dtype)


def on_device(
    count, perturbation, hours_live, start_hour, release_coeffs, batch_of_column, batch_amplitude
):
    order = perturbation.shape[1]
    columns = release_coeffs.shape[1]
    vmem = pl.BlockSpec(memory_space=pltpu.VMEM)
    smem = pl.BlockSpec(memory_space=pltpu.SMEM)
    hbm = pl.BlockSpec(memory_space=pltpu.HBM)
    f32, bf16 = jnp.float32, jnp.bfloat16
    square = (order, order)
    sems = lambda n: pltpu.SemaphoreType.DMA((2, n))
    reach, release = pl.pallas_call(
        functools.partial(kernel, count),
        out_shape=(
            jax.ShapeDtypeStruct(square, bf16),
            jax.ShapeDtypeStruct((order, columns), bf16),
        ),
        in_specs=[smem, smem, hbm, hbm, hbm, hbm],
        out_specs=(vmem, vmem),
        scratch_shapes=[
            pltpu.SMEM(batch_amplitude.shape, f32),
            pltpu.VMEM(perturbation.shape, bf16),
            pltpu.VMEM((order, columns), bf16),
            pltpu.VMEM((1, columns), jnp.int32),
            pltpu.VMEM((2,) + square, f32),
            pltpu.VMEM((2,) + square, f32),
            pltpu.VMEM(square, f32),
            pltpu.VMEM(square, f32),
            pltpu.VMEM(square, f32),
            pltpu.VMEM((order // QUAD, order), f32),
            pltpu.VMEM((order // QUAD, order), f32),
            pltpu.VMEM(square, bf16),
            pltpu.VMEM(square, bf16),
            pltpu.VMEM(square, bf16),
            pltpu.VMEM(square, bf16),
            pltpu.SemaphoreType.DMA((4,)),
            sems(QUAD),
            sems(UNITS // 2),
            sems(UNITS // 2),
            sems(UNITS // QUAD),
            sems(UNITS // QUAD),
            sems(UNITS // QUAD),
            sems(UNITS // QUAD),
            sems(UNITS // QUAD),
        ],
        compiler_params=pltpu.CompilerParams(
            collective_id=0, has_side_effects=True, vmem_limit_bytes=40 * 1024 * 1024
        ),
    )(
        hours_live,
        start_hour,
        *(
            pltpu.with_memory_space_constraint(value, pltpu.HBM)
            for value in (batch_amplitude, perturbation, release_coeffs, batch_of_column[None, :])
        ),
    )
    width = 512
    return pl.pallas_call(
        panel_tile,
        out_shape=jax.ShapeDtypeStruct((1, order, columns), bf16),
        grid=(columns // width,),
        in_specs=[vmem, pl.BlockSpec((order, width), lambda i: (0, i))],
        out_specs=pl.BlockSpec((1, order, width), lambda i: (0, 0, i)),
        compiler_params=pltpu.CompilerParams(vmem_limit_bytes=16 * 1024 * 1024),
    )(reach, release)


def solution(mesh):
    in_specs = (
        P(("basin", "tm"), None, None),
        P(("basin", "tm")),
        P(),
        P("basin", None),
        P("basin"),
        P("basin"),
    )
    out_specs = P(("basin", "tm"), None, None)
    return jax.shard_map(
        functools.partial(on_device, mesh.shape["tm"]),
        mesh=mesh,
        in_specs=in_specs,
        out_specs=out_specs,
        check_vma=False,
    )
```
